32 devices in a mesh: gx: 4 (over y, x), gy: 8 (over z, core).
Axes of the slice: x: 2, y: 2, z: 4, core: 2. Of those that a mesh axis runs over, the one named last changes fastest.
Arguments:
- input_beam: float32 [2, 4096, 4096], P(None, ('gx', 'gy')), may hold values from -6 to 6
- offsets: int32 [2], replicated, may hold values from 0 to 4096
- distances: float32 [2], replicated, may hold values from 20 to 80
- screens: int32 [1, 8192, 8192], P(None, ('gx', 'gy')), may hold values from -127 to 127
- screen_scales: float32 [1, 64, 64], replicated, may hold values from 0.005 to 0.05
- last_screen: int32 [4096, 4096], P(('gx', 'gy')), may hold values from -127 to 127
- last_scales: float32 [32, 32], replicated, may hold values from 0.005 to 0.05
Outputs:
- output_beam: float32 [2, 4096, 4096], P(None, ('gx', 'gy'))
The draws below stay inside these ranges and needn't reach their ends.
All inputs are finite; a program needn't handle non-finite values.
Results may differ from the reference program's by a relative error of at most 0.0001.
Values sent between devices are 32-bit elements; how exact they have to be, the bound alone decides.
A program may use at most 192 MiB of HBM per device.

```python
import math
import jax
import jax.numpy as jnp
from jax import lax

N = 8192
M = 4096
STEPS = 2


def plant(array, key, smallest, largest):
    longest = array.shape.index(max(array.shape))
    spots = []
    for shift in (0, 1):
        where = [jax.random.randint(jax.random.fold_in(key, axis), (), 0, length) for axis, length in enumerate(array.shape)]
        where[longest] = (where[longest] + shift) % array.shape[longest]
        spots.append(tuple(where))
    return array.at[spots[0]].set(smallest).at[spots[1]].set(largest)


def levels(rng, shape, cuts, low, top_value):
    level, own = 1.0, jax.random.fold_in(rng, 6)
    for position, shards_of in cuts:
        heights = jnp.exp(jax.random.uniform(jax.random.fold_in(own, position), (shards_of,), jnp.float32, low / len(cuts), top_value / len(cuts)))
        level = level * jnp.repeat(heights, shape[position] // shards_of).reshape([-1 if axis == position else 1 for axis in range(len(shape))])
    return level


def noise(rng, shape, width, limit, pieces=(), kind=jnp.bfloat16):
    drawn = width * jax.random.normal(rng, shape, jnp.float32)
    if pieces:
        drawn = drawn * levels(rng, shape, pieces, -0.22, 0.18)
    return jnp.clip(drawn, -limit, limit).astype(kind)


def setup_inputs(seed: int = 0) -> dict:
    key_of = jax.random.split(jax.random.key(seed), 8)
    input_beam = noise(key_of[0], (2, M, M), 1.0, 6.0, ((1, 32),), jnp.float32)
    offsets = jax.random.randint(key_of[1], (2,), 0, N - M + 1).astype(jnp.int32)
    distances = jnp.clip(jnp.exp(jax.random.uniform(key_of[2], (STEPS,), jnp.float32, math.log(20.0), math.log(80.0))), 20.0, 80.0)
    screens = plant(jax.random.randint(key_of[3], (STEPS - 1, N, N), -127, 128), jax.random.fold_in(key_of[3], 1), -127, 127).astype(jnp.int32)
    screen_scales = jnp.clip(jnp.exp(jax.random.uniform(key_of[4], (STEPS - 1, N // 128, N // 128), jnp.float32, math.log(0.005), math.log(0.05))), 0.005, 0.05)
    last_screen = plant(jax.random.randint(key_of[5], (M, M), -127, 128), jax.random.fold_in(key_of[5], 1), -127, 127).astype(jnp.int32)
    last_scales = jnp.clip(jnp.exp(jax.random.uniform(key_of[6], (M // 128, M // 128), jnp.float32, math.log(0.005), math.log(0.05))), 0.005, 0.05)
    return {"input_beam": input_beam, "offsets": offsets, "distances": distances, "screens": screens, "screen_scales": screen_scales, "last_screen": last_screen, "last_scales": last_scales}


def signed_index(length):
    indices = jnp.arange(length, dtype=jnp.int32)
    return jnp.where(indices < length // 2, indices, indices - length)


def expand_scales(scales):
    return jnp.repeat(jnp.repeat(scales, 128, axis=0), 128, axis=1)


def reference(input_beam, offsets, distances, screens, screen_scales, last_screen, last_scales):
    zero_index = jnp.zeros((), jnp.int32)
    grid = jnp.zeros((2, N, N), jnp.float32)
    grid = lax.dynamic_update_slice(grid, input_beam, (zero_index, offsets[0].astype(jnp.int32), offsets[1].astype(jnp.int32)))
    beam_field = grid[0] + 1j * grid[1]
    frequency = signed_index(N)
    squared = frequency[:, None] * frequency[:, None] + frequency[None, :] * frequency[None, :]
    squared_float = squared.astype(jnp.float32)
    phase_coef = (2.0 * math.pi / N) ** 2
    for layer_index in range(STEPS):
        spectrum = jnp.fft.fft2(beam_field)
        phases = squared_float * (distances[layer_index] * phase_coef)
        spectrum = spectrum * jnp.exp(-1j * phases)
        beam_field = jnp.fft.ifft2(spectrum)
        if layer_index < STEPS - 1:
            screen_phase = expand_scales(screen_scales[layer_index]) * screens[layer_index].astype(jnp.float32)
            beam_field = beam_field * jnp.exp(1j * screen_phase)
    crop_start = (N - M) // 2
    window = beam_field[crop_start:crop_start + M, crop_start:crop_start + M]
    last_phase = expand_scales(last_scales) * last_screen.astype(jnp.float32)
    window = window * jnp.exp(1j * last_phase)
    return jnp.stack([jnp.real(window), jnp.imag(window)]).astype(jnp.float32)
```

```python
import math

import jax
import jax.numpy as jnp
from jax import lax
from jax.experimental import pallas as pl
from jax.experimental.pallas import tpu as pltpu
from jax.sharding import PartitionSpec as P

AXES = ("gx", "gy")
INNER = 128


def contract(pattern, lhs_array, rhs_array, precision=lax.Precision.HIGH):
    return jnp.einsum(
        pattern, lhs_array, rhs_array, precision=precision, preferred_element_type=jnp.float32
    )


def unit_angles(product, length):
    angles = (product % length).astype(jnp.float32) * (2.0 * math.pi / length)
    return jnp.cos(angles), jnp.sin(angles)


def operator_lags(distance, shift, length):
    outer = length // INNER
    k_ids = jnp.arange(outer, dtype=jnp.int32)
    m_ids = jnp.arange(INNER, dtype=jnp.int32)
    index = k_ids[:, None] + outer * m_ids[None, :]
    signed = jnp.where(index < length // 2, index, index - length)
    phases = (signed * signed).astype(jnp.float32) * (
        distance * ((2.0 * math.pi / length) ** 2)
    )
    phase_re, phase_im = jnp.cos(phases), -jnp.sin(phases)
    shift_re, shift_im = unit_angles(index * shift, length)
    filt_re = phase_re * shift_re - phase_im * shift_im
    filt_im = phase_re * shift_im + phase_im * shift_re
    lag_ids = jnp.arange(2 * INNER, dtype=jnp.int32)
    lags = jnp.where(lag_ids < INNER, lag_ids, lag_ids - 2 * INNER)
    table_re, table_im = unit_angles(m_ids[:, None] * lags[None, :], INNER)
    best = lax.Precision.HIGHEST
    sum_re = contract("km,md->kd", filt_re, table_re, best) - contract(
        "km,md->kd", filt_im, table_im, best
    )
    sum_im = contract("km,md->kd", filt_re, table_im, best) + contract(
        "km,md->kd", filt_im, table_re, best
    )
    twist_re, twist_im = unit_angles(k_ids[:, None] * lags[None, :], length)
    scale = 1.0 / length
    return (
        (sum_re * twist_re - sum_im * twist_im) * scale,
        (sum_re * twist_im + sum_im * twist_re) * scale,
    )


def toeplitz_kernel(lag_re_ref, lag_im_ref, out_ref):
    for slot in range(lag_re_ref.shape[0]):
        parts = []
        for lag_ref in (lag_re_ref, lag_im_ref):
            wide = jnp.broadcast_to(lag_ref[slot, :][None, :], (INNER, 2 * INNER))
            parts.append(pltpu.roll(wide, 0, 1, stride=1, stride_axis=0)[:, :INNER])
        out_ref[slot, :INNER, :INNER] = parts[0]
        out_ref[slot, :INNER, INNER:] = parts[1]
        out_ref[slot, INNER:, :INNER] = -parts[1]
        out_ref[slot, INNER:, INNER:] = parts[0]


def toeplitz(lag_re, lag_im):
    outer = lag_re.shape[0]
    block = 8
    return pl.pallas_call(
        toeplitz_kernel,
        grid=(outer // block,),
        in_specs=[pl.BlockSpec((block, 2 * INNER), lambda step: (step, 0))] * 2,
        out_specs=pl.BlockSpec((block, 2 * INNER, 2 * INNER), lambda step: (step, 0, 0)),
        out_shape=jax.ShapeDtypeStruct((outer, 2 * INNER, 2 * INNER), jnp.float32),
    )(lag_re, lag_im)


def embed(real_part, imag_part, axis_in, axis_out):
    top = jnp.stack([real_part, imag_part], axis=axis_out)
    low = jnp.stack([-imag_part, real_part], axis=axis_out)
    return jnp.stack([top, low], axis=axis_in)


def propagate(planes, distance, shift, length, out_outer):
    outer = length // INNER
    in_outer = planes.shape[2]
    ids = jnp.arange(outer, dtype=jnp.int32)
    dft_re, dft_im = unit_angles(ids[:, None] * ids[None, :], outer)
    first = embed(dft_re[:in_outer], -dft_im[:in_outer], 0, 1)
    last = embed(dft_re[:, :out_outer], dft_im[:, :out_outer], 0, 1)
    lag_re, lag_im = operator_lags(distance, shift, length)
    middle = toeplitz(lag_re, lag_im).reshape((outer, 2, INNER, 2, INNER))
    spectral = contract("cbpq,cpdk->kbdq", planes, first)
    mixed = contract("kbdq,kdqes->kbes", spectral, middle)
    return contract("kbes,ekfp->fbps", mixed, last)


def move(blocks):
    return lax.all_to_all(blocks, AXES, split_axis=1, concat_axis=1, tiled=True)


def to_columns(planes, devices_total):
    count, row_count, width = planes.shape
    col_count = width // devices_total
    blocks = planes.reshape((count, row_count, devices_total, col_count)).transpose((0, 2, 3, 1))
    arrived = move(blocks.reshape((count, devices_total, col_count * row_count)))
    arrived = arrived.reshape((count, devices_total, col_count, row_count)).transpose((0, 2, 1, 3))
    return arrived.reshape((count, col_count, devices_total * row_count))


def to_rows(planes, devices_total):
    count, col_count, height = planes.shape
    row_count = height // devices_total
    blocks = planes.reshape((count, col_count, devices_total, row_count)).transpose((0, 2, 1, 3))
    arrived = move(blocks.reshape((count, devices_total, col_count * row_count)))
    arrived = arrived.reshape((count, devices_total, col_count, row_count)).transpose((0, 3, 1, 2))
    return arrived.reshape((count, row_count, devices_total * col_count))


def pick_scales(scales, first, count):
    block_ids = (first + jnp.arange(count, dtype=jnp.int32)) // 128
    onehot = (
        block_ids[:, None] == jnp.arange(scales.shape[0], dtype=jnp.int32)[None, :]
    ).astype(jnp.float32)
    return jnp.dot(
        onehot, scales, precision=lax.Precision.HIGHEST, preferred_element_type=jnp.float32
    )


def rotate_planes(planes, phases):
    cosine = jnp.cos(phases)
    sine = jnp.sin(phases)
    return jnp.stack([planes[0] * cosine - planes[1] * sine, planes[0] * sine + planes[1] * cosine])


def body(input_beam, offsets, distances, screens, screen_scales, last_screen, last_scales):
    devices_total = lax.axis_size(AXES)
    position = lax.axis_index(AXES)
    length = screens.shape[2]
    window = input_beam.shape[2]
    rows = input_beam.shape[1]
    outer = length // INNER
    window_outer = window // INNER
    cols = length // devices_total
    steps = distances.shape[0]
    crop = (length - window) // 2
    flat_screens = [to_columns(screens[s : s + 1], devices_total)[0] for s in range(steps - 1)]
    field = propagate(
        input_beam.reshape((2, rows, window_outer, INNER)), distances[0], -offsets[1], length, outer
    )
    field = to_columns(field.reshape((2, rows, length)), devices_total)
    field = field.reshape((2, cols, window_outer, INNER))
    for step in range(steps):
        final = step == steps - 1
        shift = jnp.zeros((), jnp.int32)
        if step == 0:
            shift = shift - offsets[0]
        if final:
            shift = shift + crop
        field = propagate(
            field, distances[step], shift, length, window_outer if final else outer
        )
        if not final:
            phases = pick_scales(screen_scales[step].T, position * cols, cols)[
                :, :, None
            ] * flat_screens[step].reshape((cols, outer, INNER)).astype(jnp.float32)
            field = rotate_planes(field, phases)
    field = to_rows(field.reshape((2, cols, window)), devices_total)
    field = propagate(
        field.reshape((2, rows, outer, INNER)),
        distances[steps - 1],
        jnp.full((), crop, jnp.int32),
        length,
        window_outer,
    )
    phases = pick_scales(last_scales, position * rows, rows)[:, :, None] * last_screen.reshape(
        (rows, window_outer, INNER)
    ).astype(jnp.float32)
    return rotate_planes(field, phases).reshape((2, rows, window))


def solution(mesh):
    return jax.shard_map(
        body,
        mesh=mesh,
        in_specs=(
            P(None, AXES, None),
            P(),
            P(),
            P(None, AXES, None),
            P(),
            P(AXES, None),
            P(),
        ),
        out_specs=P(None, AXES, None),
        check_vma=False,
    )
```
